32 devices in a mesh: mem: 4 (over x, core), lat: 4 (over z), lon: 2 (over y).
Axes of the slice: x: 2, y: 2, z: 4, core: 2. Of those that a mesh axis runs over, the one named last changes fastest.
Arguments:
- initial_temp: float32 [100, 8, 512], P(None, 'lon', 'lat'), may hold values from -6 to 6
- land_mask: int32 [8, 512], P('lon', 'lat'), may hold values 0 or 1
- pert_table: float32 [16, 100], replicated, may hold values from 0.03 to 0.24
- pert_index: int32 [8], P('mem'), may hold values from 0 to 15
- base_kh: float32 [100], replicated, may hold values from 0.03 to 0.24
- member_mix: bfloat16 [8, 100, 100], P('mem'), may hold values from -0.15625 to 0.15625
- base_mix: bfloat16 [100, 100], replicated, may hold values from -0.15625 to 0.15625
- owner: int32 [2048, 1], P(('lat', 'lon')), may hold values from 0 to 7; in each aligned block of 256 rows (0 to 255, 256 to 511, ...) at most 64 rows name the same one
- column: int32 [2048], P(('lat', 'lon')), may hold values from 0 to 511
- interp_w: float32 [2048, 100], P(('lat', 'lon')), may hold values from 0 to 1
- obs_inv_var: float32 [2048, 100], P(('lat', 'lon')), may hold values from 1 to 16
- observed: float32 [2048, 100], P(('lat', 'lon')), may hold values from -6 to 6
Outputs:
- member_temp: bfloat16 [8, 100, 8, 512], P('mem', None, 'lon', 'lat')
- base_temp: bfloat16 [100, 8, 512], P(None, 'lon', 'lat')
- gram_block: float32 [8, 8], replicated
- projection: float32 [8], replicated
- misfit: float32 [2048, 100], P(('lat', 'lon'))
The draws below stay inside these ranges and needn't reach their ends.
Inputs may be any that keep to these rules, and one draw needn't show every extreme that they name: Within the records of one device no owner is named more than 64 times, and in every draw some owner is named exactly 64 times by some device's records. The column within the owner's block is the longitude offset times 128 plus the latitude offset.
All inputs are finite; a program needn't handle non-finite values. No bound on the sum of `land_mask` on one device may be relied on, other than what follows from the above.
Results may differ from the reference program's by a relative error of at most 0.012.
Values may be sent and summed in bfloat16 or wider, within the bound.
A program may use at most 64 MiB of HBM per device.

```python
import math
import jax
import jax.numpy as jnp
import numpy as np
from jax import lax

K = 100
CX = 4
CY = 128
PROF_DEV = 256
STEPS = 5
NPERT = 16
MEMBERS = 8
LON = 8
LAT = 512
CAP = 64
PROFILES = 2048
N_LAT = 4
N_LON = 2


def touch_ends(entries, own_key, low, top_value):
    longest = entries.shape.index(max(entries.shape))
    spots = []
    for shift in (0, 1):
        where = [jax.random.randint(jax.random.fold_in(own_key, axis), (), 0, length) for axis, length in enumerate(entries.shape)]
        where[longest] = (where[longest] + shift) % entries.shape[longest]
        spots.append(tuple(where))
    return entries.at[spots[0]].set(low).at[spots[1]].set(top_value)


def shard_levels(stream_key, shape, shards, least, largest):
    factor_of = 1.0
    for position, shards_of in shards:
        heights = jax.random.uniform(jax.random.fold_in(jax.random.fold_in(stream_key, 6), position), (shards_of,), jnp.float32, least / len(shards), largest / len(shards))
        factor_of = factor_of * jnp.repeat(jnp.exp(heights), shape[position] // shards_of).reshape((-1,) + (1,) * (len(shape) - 1 - position))
    return factor_of


def deal_out(stream_key, own, number, rows, count, top, most, lean):
    sequence = jax.random.permutation(stream_key, count)
    heavy_load, ordinary = portions_of(count, rows * top, most, lean, True), portions_of(count, rows * top, most, lean, False)
    places = jnp.arange(count)

    def named(lengths, turn):
        used = int((lengths > 0).sum())
        fixed = max(1, used // 4)
        shifted = fixed + (places - fixed + turn * (used - fixed)) % max(1, count - fixed)
        return jnp.zeros((count,), jnp.int32).at[sequence[jnp.where(places < fixed, places, shifted)]].set(jnp.asarray(lengths, jnp.int32))

    lengths = jnp.where(number % 4 == 0, named(heavy_load, number // 4), named(ordinary, number - number // 4 - 1))
    mixed = jax.random.permutation(jax.random.fold_in(own, 3), count)
    source_of, taker = mixed[0:count // 2 * 2:2], mixed[1:count // 2 * 2:2]
    margin = jnp.minimum(lengths[source_of] - 1, most - lengths[taker]) // 2
    margin = jnp.where((source_of == sequence[0]) | (taker == sequence[0]) | (lengths[taker] == 0), 0, jnp.maximum(margin, 0))
    shifted = jax.random.randint(jax.random.fold_in(own, 4), (count // 2,), 0, 1 << 20) % (margin + 1)
    lengths = lengths.at[source_of].add(-shifted).at[taker].add(shifted)
    labels = jnp.searchsorted(jnp.cumsum(lengths), jnp.arange(rows * top), side="right").astype(jnp.int32)
    listing = labels.reshape(top, rows).T
    listing = listing[jax.random.permutation(jax.random.fold_in(own, 1), rows)]
    turn = jax.random.randint(jax.random.fold_in(own, 2), (rows, 1), 0, top)
    return jnp.take_along_axis(listing, (jnp.arange(top)[None, :] + turn) % top, axis=1)


def portions_of(amount, total, most, skew, full):
    loads = [(1 << 20) // math.isqrt(rank ** skew) + 1 for rank in range(1, amount + 1)]
    largest = most if full else min(most, max(-(-total // amount), total * loads[0] // sum(loads)))
    least = 1 if total - largest >= amount - 1 else 0
    given, surplus = [largest] + [least] * (amount - 1), total - largest - least * (amount - 1)
    while surplus > 0:
        candidates = [i for i in range(1, amount) if given[i] < largest] or [i for i in range(1, amount) if given[i] < most]
        mass, left = sum([loads[i] for i in candidates]), surplus
        for i in candidates:
            addition = min(most - given[i], max(1, left * loads[i] // mass), surplus)
            given[i] = given[i] + addition
            surplus = surplus - addition
    return np.array(given)


def noise(stream_key, extent, width, bound, split=(), dtype=jnp.bfloat16):
    drawn = width * jax.random.normal(stream_key, extent, jnp.float32)
    if split:
        drawn = drawn * shard_levels(stream_key, extent, split, -0.22, 0.18)
    return jnp.clip(drawn, -bound, bound).astype(dtype)


def setup_inputs(seed: int = 0) -> dict:
    arg_keys = jax.random.split(jax.random.key(seed), 13)
    initial_temp = noise(arg_keys[0], (K, LON, LAT), 1.0, 6.0, ((1, 2), (2, 4)), jnp.float32)
    land_mask = touch_ends((jax.random.randint(arg_keys[1], (LON, LAT), 0, 5) < 4).astype(jnp.int32), jax.random.fold_in(arg_keys[1], 1), 0, 1)
    pert_table = jnp.clip(jnp.exp(jax.random.uniform(arg_keys[2], (NPERT, K), jnp.float32, math.log(0.03), math.log(0.24))), 0.03, 0.24)
    pert_index = touch_ends(jax.random.randint(arg_keys[3], (MEMBERS,), 0, NPERT), jax.random.fold_in(arg_keys[3], 1), 0, NPERT - 1).astype(jnp.int32)
    base_kh = jnp.clip(jnp.exp(jax.random.uniform(arg_keys[4], (K,), jnp.float32, math.log(0.03), math.log(0.24))), 0.03, 0.24)
    member_mix = noise(arg_keys[5], (MEMBERS, K, K), (16 * K) ** -0.5, 0.15625, ((0, 4),))
    base_mix = noise(arg_keys[6], (K, K), (16 * K) ** -0.5, 0.15625)
    owner_keys = jax.random.split(jax.random.fold_in(arg_keys[7], 1), PROFILES // PROF_DEV)
    owner_turns = jax.random.permutation(jax.random.fold_in(arg_keys[7], 3), PROFILES // PROF_DEV)
    owner = jax.vmap(lambda own, number: deal_out(jax.random.fold_in(arg_keys[7], 2), own, number, PROF_DEV, N_LAT * N_LON, 1, CAP, 2))(owner_keys, owner_turns).reshape((PROFILES, 1))
    column = touch_ends(jax.random.randint(arg_keys[8], (PROFILES,), 0, CX * CY), jax.random.fold_in(arg_keys[8], 1), 0, (CX * CY) - 1).astype(jnp.int32)
    interp_w = jnp.clip(1.0 * jax.random.uniform(arg_keys[9], (PROFILES, K), jnp.float32) ** shard_levels(arg_keys[9], (PROFILES, K), ((0, 8),), -0.2, 0.2), 0.0, 1.0)
    obs_inv_var = jnp.clip(jnp.exp(math.log(16.0) - 2.7725887 * jax.random.uniform(arg_keys[10], (PROFILES, K), jnp.float32) ** shard_levels(arg_keys[10], (PROFILES, K), ((0, 8),), -0.2, 0.2)), 1.0, 16.0)
    observed = noise(arg_keys[11], (PROFILES, K), 1.0, 6.0, ((0, 8),), jnp.float32)
    return dict(initial_temp=initial_temp, land_mask=land_mask, pert_table=pert_table, pert_index=pert_index, base_kh=base_kh, member_mix=member_mix, base_mix=base_mix, owner=owner, column=column, interp_w=interp_w, obs_inv_var=obs_inv_var, observed=observed)


def advance_run(fields, kh_profile, mixing, ocean_open, has_next, has_prior):
    values = fields.astype(jnp.float32)
    laplace = jnp.roll(values, -1, 1) + jnp.roll(values, 1, 1) - 2.0 * values
    laplace = laplace + has_next * (jnp.roll(values, -1, 2) - values) + has_prior * (jnp.roll(values, 1, 2) - values)
    right_side = (values + kh_profile[:, None, None] * laplace).astype(jnp.bfloat16)
    right_float = right_side.astype(jnp.float32)
    vertical = right_float + jnp.einsum("kj,jab->kab", mixing.astype(jnp.float32), right_float, precision=lax.Precision.HIGHEST)
    return (values + ocean_open * (vertical - values)).astype(jnp.bfloat16)


def reference(initial_temp, land_mask, pert_table, pert_index, base_kh, member_mix, base_mix, owner, column, interp_w, obs_inv_var, observed):
    kh_runs = jnp.concatenate([pert_table[pert_index], base_kh[None, :]], 0)
    mix_runs = jnp.concatenate([member_mix, base_mix[None]], 0)
    ocean_open = land_mask.astype(jnp.float32)
    lat_rows = jnp.arange(LAT)
    has_next = (lat_rows < LAT - 1).astype(jnp.float32)
    has_prior = (lat_rows > 0).astype(jnp.float32)

    def run_one(pair):
        kh_profile, mixing = pair
        fields = initial_temp.astype(jnp.bfloat16)
        for step_index in range(STEPS):
            fields = advance_run(fields, kh_profile, mixing, ocean_open, has_next, has_prior)
        return fields

    finals = lax.map(run_one, (kh_runs, mix_runs))
    run_count = MEMBERS + 1
    target = owner[:, 0]
    lat_block = target // N_LON
    lon_block = target % N_LON
    global_lon = lon_block * CX + column // CY
    global_lat = lat_block * CY + column % CY
    column_flat = (global_lon * LAT + global_lat).astype(jnp.int32)
    picked = jnp.take(finals.reshape(run_count, K, LON * LAT), column_flat, axis=2).astype(jnp.float32)
    deeper = jnp.concatenate([picked[:, 1:], picked[:, -1:]], 1)
    weight = interp_w.T
    modeled = weight * picked + (1.0 - weight) * deeper
    green_cols = (modeled[:MEMBERS] - modeled[MEMBERS]).astype(jnp.bfloat16).astype(jnp.float32)
    misfit = observed.T - modeled[MEMBERS]
    normalizer = 1.0 / (PROFILES * K)
    weighted = green_cols * obs_inv_var.T
    gram_block = jnp.einsum("mkp,nkp->mn", weighted, green_cols, precision=lax.Precision.HIGHEST) * normalizer
    projection = jnp.einsum("mkp,kp->m", weighted, misfit, precision=lax.Precision.HIGHEST) * normalizer
    return finals[:MEMBERS], finals[MEMBERS], gram_block, projection, misfit.T
```

```python
import functools

import jax
import jax.numpy as jnp
import numpy as np
from jax import lax
from jax.experimental import pallas as pl
from jax.experimental.pallas import tpu as pltpu
from jax.sharding import PartitionSpec as P

STEPS = 5
SIDE = 8
CELL = 2 * SIDE
MESH = pl.DeviceIdType.MESH
BF, F32, I32 = jnp.bfloat16, jnp.float32, jnp.int32


def up(value, multiple):
    return -(-value // multiple) * multiple


def offsets_of(lon_count, width):
    reach = -(-STEPS // width)
    if 2 * reach + 1 >= lon_count:
        return list(range(lon_count)), True
    return list(range(-reach, reach + 1)), False


def lat_blocks(columns, ring, length):
    per = 128 // CELL
    halo_tiles = -(-columns // per)
    total = columns + halo_tiles

    def where(col, lat):
        if 0 <= lat < length:
            return col * length + lat
        inside = lat + SIDE if lat < 0 else lat - length + SIDE
        return (columns + col // per) * 128 + (col % per) * CELL + inside

    matrix = {}

    def put(source, target, amount):
        key = (source // 128, target // 128)
        block = matrix.setdefault(key, np.zeros((128, 128), np.float32))
        block[source % 128, target % 128] += amount

    for col in range(columns):
        for lat in range(-SIDE, length + SIDE):
            target = where(col, lat)
            put(target, target, -4.0)
            for step in (-1, 1):
                if -SIDE <= lat + step < length + SIDE:
                    put(where(col, lat + step), target, 1.0)
                near = col + step
                if ring:
                    near %= columns
                if 0 <= near < columns and not 0 <= lat < length:
                    put(where(near, lat), target, 1.0)
    plans, stacked = [], []
    for tile in range(total):
        sources = [s for s in range(total) if (s, tile) in matrix]
        start = sum(b.shape[0] for b in stacked)
        stacked += [matrix[(s, tile)] for s in sources]
        plans.append((sources, start))
    return plans, np.concatenate(stacked, 0)


def coords(linear, lat_count, lon_count):
    plane = lat_count * lon_count
    rest = linear % plane
    return linear // plane, rest // lon_count, rest % lon_count


def exchange_kernel(
    sizes, main_ref, edge_ref, owner_ref, column_ref, near_ref, halo_ref, ids_ref,
    main_send, main_recv, halo_send, halo_recv, ids_send, ids_recv,
):
    lat_count, lon_count, offsets, slots = sizes
    owners = lat_count * lon_count
    lat, lon = lax.axis_index("lat"), lax.axis_index("lon")
    me = lat * lon_count + lon
    barrier = pltpu.get_barrier_semaphore()

    def place(d):
        ll = (me + d) % owners
        return {"lat": ll // lon_count, "lon": ll % lon_count}

    def greet(d, carry):
        pl.semaphore_signal(barrier, inc=1, device_id=place(d), device_id_type=MESH)
        return carry

    lax.fori_loop(1, owners, greet, 0)

    records = owner_ref.shape[1]
    target = owner_ref[...]
    match = (lax.broadcasted_iota(I32, (up(owners, 16), records), 0) == target).astype(BF)
    before = (
        lax.broadcasted_iota(I32, (records, records), 0)
        < lax.broadcasted_iota(I32, (records, records), 1)
    ).astype(BF)
    earlier = jnp.dot(match, before, preferred_element_type=F32)
    rank = jnp.sum(earlier * match.astype(F32), axis=0, keepdims=True)
    position = target.astype(F32) * slots + rank
    row = lax.broadcasted_iota(I32, (8, records), 0)
    ids_ref[me] = jnp.where(row == 0, position, column_ref[...].astype(F32) + 1.0)
    pl.semaphore_wait(barrier, owners - 1)

    copies = []
    near = 0
    for index, offset in enumerate(offsets):
        to_lon = (lon - offset + lon_count) % lon_count
        if offset != 0:
            copies.append(
                pltpu.make_async_remote_copy(
                    main_ref, near_ref.at[near], main_send.at[near], main_recv.at[near],
                    device_id={"lat": lat, "lon": to_lon}, device_id_type=MESH,
                )
            )
            near += 1
        for side, step in ((0, 1), (1, lat_count - 1)):
            copies.append(
                pltpu.make_async_remote_copy(
                    edge_ref, halo_ref.at[index, side],
                    halo_send.at[index, side], halo_recv.at[index, side],
                    device_id={"lat": (lat + step) % lat_count, "lon": to_lon},
                    device_id_type=MESH,
                )
            )
    for copy in copies:
        copy.start()

    def ids_copy(d):
        return pltpu.make_async_remote_copy(
            ids_ref.at[me], ids_ref.at[me], ids_send.at[d - 1], ids_recv.at[d - 1],
            device_id=place(d), device_id_type=MESH,
        )

    def send_ids(d, carry):
        ids_copy(d).start()
        return carry

    lax.fori_loop(1, owners, send_ids, 0)

    def wait_ids(d, carry):
        source = (me + owners - d) % owners
        ids_copy(d).wait_send()
        pltpu.make_async_remote_copy(
            ids_ref.at[source], ids_ref.at[source], ids_send.at[d - 1], ids_recv.at[d - 1],
            device_id=place(d), device_id_type=MESH,
        ).wait_recv()
        return carry

    lax.fori_loop(1, owners, wait_ids, 0)
    for copy in copies:
        copy.wait()


def steps_kernel(
    sizes, plans, pert_index, main_ref, near_ref, halo_ref, ids_ref, blocks_ref, table_ref,
    base_kh_ref, mix_ref, base_mix_ref, fields_ref, picks_ref, base_ref, v_ref, rs_ref, f_ref,
):
    lat_count, lon_count, offsets, ring, slots, mem_count = sizes
    owners = lat_count * lon_count
    lat = lax.axis_index("lat")
    me = lat * lon_count + lax.axis_index("lon")
    rows = main_ref.shape[0]
    levels = table_ref.shape[1]
    own = main_ref.shape[1]
    runs = mix_ref.shape[0] + 1
    columns = len(offsets) * (own // 128)
    total = len(plans)
    first = offsets.index(0) * own
    lane = lax.broadcasted_iota(I32, (1, 128), 1)

    near = 0
    for index, offset in enumerate(offsets):
        if offset == 0:
            block = main_ref[...]
        else:
            block = near_ref[near]
            near += 1
        for run in range(runs):
            v_ref[run * rows : (run + 1) * rows, index * own : (index + 1) * own] = block
    low = lane % CELL < SIDE
    lanes = own // 128 * CELL
    per = 128 // lanes
    for tile in range(total - columns):
        value = jnp.zeros((rows, 128), F32)
        for part in range(per):
            index = tile * per + part
            if index >= len(offsets):
                continue
            prior = jnp.where(lat > 0, halo_ref[index, 0].astype(F32), 0.0)
            later = jnp.where(lat < lat_count - 1, halo_ref[index, 1].astype(F32), 0.0)
            both = jnp.where(low, prior, later)
            if part:
                both = pltpu.roll(both, part * lanes, 1)
            value = jnp.where((lane >= part * lanes) & (lane < (part + 1) * lanes), both, value)
        at = (columns + tile) * 128
        for run in range(runs):
            v_ref[run * rows : (run + 1) * rows, at : at + 128] = value.astype(BF)

    tail = v_ref[levels // 16 * 16 : levels // 16 * 16 + 16, :].astype(F32)
    open_row = tail[levels % 16 : levels % 16 + 1, :]

    def column_of(row):
        eye = lax.broadcasted_iota(I32, (rows, levels), 0) == lax.broadcasted_iota(
            I32, (rows, levels), 1
        )
        return jnp.sum(jnp.where(eye, row, 0.0), axis=1, keepdims=True)

    kh = [column_of(table_ref[pl.ds(pert_index[r], 1), :]) for r in range(runs - 1)]
    kh = jnp.concatenate(kh + [column_of(base_kh_ref[...])], 0)
    at_start = jnp.where(lat == 0, 1.0, 0.0)
    at_end = jnp.where(lat == lat_count - 1, 1.0, 0.0)
    edge = jnp.where(lane == 0, at_start, 0.0) + jnp.where(lane == 127, at_end, 0.0)

    def step(number, carry):
        for tile in range(total):
            sources, start = plans[tile]
            left = jnp.concatenate([v_ref[:, s * 128 : (s + 1) * 128] for s in sources], 1)
            right = blocks_ref[start : start + 128 * len(sources), :]
            laplace = jnp.dot(left, right, preferred_element_type=F32)
            values = v_ref[:, tile * 128 : (tile + 1) * 128].astype(F32)
            if tile < columns:
                for shift in (-1, 1):
                    other = tile + shift
                    if ring:
                        other %= columns
                    if 0 <= other < columns:
                        laplace += v_ref[:, other * 128 : (other + 1) * 128].astype(F32)
                laplace += edge * values
            rs_ref[:, tile * 128 : (tile + 1) * 128] = (values + kh * laplace).astype(BF)
        for run in range(runs):
            mix = mix_ref[run] if run < runs - 1 else base_mix_ref[...]
            top = run * rows
            for start in range(0, total, 3):
                end = min(start + 3, total)
                part = slice(start * 128, end * 128)
                right_side = rs_ref[top : top + levels, part]
                vertical = right_side.astype(F32) + jnp.dot(
                    mix, right_side, preferred_element_type=F32
                )
                values = v_ref[top : top + levels, part].astype(F32)
                v_ref[top : top + levels, part] = jnp.where(
                    open_row[:, part] > 0.5, vertical, values
                ).astype(BF)
        return carry

    lax.fori_loop(0, STEPS, step, 0)

    f_ref[...] = jnp.zeros_like(f_ref)
    for run in range(runs):
        block = v_ref[run * rows : (run + 1) * rows, first : first + own]
        fields_ref[run] = block
        f_ref[run * 128 : run * 128 + rows, :] = block

    each = slots // mem_count
    records = ids_ref.shape[2]
    fields = f_ref[...]

    def pick(source, carry):
        known = ids_ref[source]
        slot = lax.broadcasted_iota(I32, (slots, records), 0) + me * slots
        chosen = jnp.where(slot.astype(F32) == known[0:1], known[1:2], 0.0)
        cell = jnp.sum(chosen, axis=1, keepdims=True) - 1.0
        lanes_own = lax.broadcasted_iota(I32, (slots, own), 1).astype(F32)
        hot = jnp.where(lanes_own == cell, 1.0, 0.0).astype(BF)
        got = lax.dot_general(
            hot, fields, (((1,), (1,)), ((), ())), preferred_element_type=F32
        ).astype(BF)
        for run in range(runs - 1):
            for j in range(mem_count):
                picks_ref[source, j, run] = got[
                    j * each : (j + 1) * each, run * 128 : (run + 1) * 128
                ]
        base_ref[source] = got[:, (runs - 1) * 128 :]
        return carry

    lax.fori_loop(0, owners, pick, 0)


def gram_kernel(
    sizes, picks_ref, base_ref, ids_ref, owner_ref, w_ref, inv_ref, obs_ref, sum_ref, misfit_ref,
    got_ref, base_got, tiles_ref, got_send, got_recv, base_send, base_recv, sum_send, sum_recv,
):
    mem_count, lat_count, lon_count, slots = sizes
    owners = lat_count * lon_count
    world = mem_count * owners
    mem = lax.axis_index("mem")
    lat, lon = lax.axis_index("lat"), lax.axis_index("lon")
    plane = lat * lon_count + lon
    me = mem * owners + plane
    barrier = pltpu.get_barrier_semaphore()
    records, levels = w_ref.shape
    each = slots // mem_count
    local = picks_ref.shape[2]
    members = local * mem_count

    def device(linear):
        where = coords(linear, lat_count, lon_count)
        return {"mem": where[0], "lat": where[1], "lon": where[2]}

    def greet(d, carry):
        pl.semaphore_signal(
            barrier, inc=1, device_id=device((me + d) % world), device_id_type=MESH
        )
        return carry

    lax.fori_loop(1, world, greet, 0)
    got_ref[me] = picks_ref[plane, mem]
    base_got[plane] = base_ref[plane]
    pl.semaphore_wait(barrier, world - 1)

    def got_copy(d, slot):
        to = (me + d) % world
        return pltpu.make_async_remote_copy(
            picks_ref.at[to % owners, to // owners], got_ref.at[slot],
            got_send.at[d - 1], got_recv.at[d - 1],
            device_id=device(to), device_id_type=MESH,
        )

    def base_copy(d, slot):
        to = (plane + d) % owners
        return pltpu.make_async_remote_copy(
            base_ref.at[to], base_got.at[slot], base_send.at[d - 1], base_recv.at[d - 1],
            device_id=device(mem * owners + to), device_id_type=MESH,
        )

    def start_base(d, carry):
        base_copy(d, plane).start()
        return carry

    def start_got(d, carry):
        got_copy(d, me).start()
        return carry

    lax.fori_loop(1, owners, start_base, 0)
    lax.fori_loop(1, world, start_got, 0)

    target = owner_ref[...]
    match = (lax.broadcasted_iota(I32, (records, up(owners, 128)), 1) == target).astype(BF)
    before = (
        lax.broadcasted_iota(I32, (records, records), 1)
        < lax.broadcasted_iota(I32, (records, records), 0)
    ).astype(BF)
    earlier = jnp.dot(before, match, preferred_element_type=F32)
    rank = jnp.sum(earlier * match.astype(F32), axis=1, keepdims=True)
    position = target.astype(F32) * slots + rank
    position_row = ids_ref[plane][0:1]
    group = 8 if owners % 8 == 0 else owners
    wide = group * each

    def slot_values(chunk):
        slot = (
            (lax.broadcasted_iota(I32, (group, each, records), 0) + chunk * group) * slots
            + lax.broadcasted_iota(I32, (group, each, records), 1)
            + mem * each
        ).reshape(wide, records)
        hot = jnp.where(slot.astype(F32) == position_row, 1.0, 0.0)
        return [
            jnp.dot(hot, ref[...], precision=lax.Precision.HIGHEST, preferred_element_type=F32)
            for ref in (w_ref, inv_ref, obs_ref)
        ]

    lane = lax.broadcasted_iota(I32, (1, 128), 1)

    def interpolated(value, weight):
        deeper = jnp.where(lane == levels - 1, value, pltpu.roll(value, 127, 1))
        return weight * value[:, :levels] + (1.0 - weight) * deeper[:, :levels]

    early = slot_values(0) if owners == group else None

    def wait_base(d, carry):
        base_copy(d, (plane + owners - d) % owners).wait()
        return carry

    lax.fori_loop(1, owners, wait_base, 0)

    def spread(chunk, total):
        cells = base_got[pl.ds(chunk * group, group)].reshape(group * slots, 128)
        at = lax.broadcasted_iota(I32, (records, group * slots), 1) + chunk * (group * slots)
        hot = jnp.where(at.astype(F32) == position, 1.0, 0.0).astype(BF)
        return total + jnp.dot(hot, cells, preferred_element_type=F32)

    picked = jnp.zeros((records, 128), F32)
    if owners == group:
        picked = spread(0, picked)
    else:
        picked = lax.fori_loop(0, owners // group, spread, picked)
    misfit_ref[...] = obs_ref[...] - interpolated(picked, w_ref[...])

    def wait_got(d, carry):
        got_copy(d, (me + world - d) % world).wait()
        return carry

    lax.fori_loop(1, world, wait_got, 0)

    def gram(chunk, total):
        weight, inv_var, measured = slot_values(chunk) if early is None else early
        base = base_got[pl.ds(chunk * group, group), pl.ds(mem * each, each)]
        base = interpolated(base.reshape(wide, 128).astype(F32), weight)
        others = []
        for m in range(members):
            start = (m // local) * owners + chunk * group
            cells = got_ref[pl.ds(start, group), m % local].reshape(wide, 128).astype(F32)
            green = interpolated(cells, weight) - base
            others.append(green.astype(BF).astype(F32))
        others.append(measured - base)
        lines = []
        for m in range(members):
            weighted = others[m] * inv_var
            for n in range(members + 1):
                if n < m:
                    lines.append(lines[n * 16 + m])
                else:
                    lines.append(jnp.sum(weighted * others[n], axis=0, keepdims=True))
            lines += [jnp.zeros((1, levels), F32)] * (16 - members - 1)
        return total + jnp.concatenate(lines, 0)

    total = jnp.zeros((members * 16, levels), F32)
    if owners == group:
        total = gram(0, total)
    else:
        total = lax.fori_loop(0, owners // group, gram, total)
    sums = jnp.sum(total, axis=1, keepdims=True)
    spot = lax.broadcasted_iota(I32, (members, 16, 128), 1) == lax.broadcasted_iota(
        I32, (members, 16, 128), 2
    )
    tile = jnp.sum(jnp.where(spot, sums.reshape(members, 16, 1), 0.0), axis=1)
    tiles_ref[me] = tile

    def sum_copy(d, slot):
        return pltpu.make_async_remote_copy(
            tiles_ref.at[slot], tiles_ref.at[slot], sum_send.at[d - 1], sum_recv.at[d - 1],
            device_id=device((me + d) % world), device_id_type=MESH,
        )

    def start_sum(d, carry):
        sum_copy(d, me).start()
        return carry

    def wait_sum(d, carry):
        sum_copy(d, me).wait_send()
        sum_copy(d, (me + world - d) % world).wait_recv()
        return carry

    lax.fori_loop(1, world, start_sum, 0)
    lax.fori_loop(1, world, wait_sum, 0)
    sum_ref[...] = jnp.sum(tiles_ref[...], axis=0) * (1.0 / (records * owners * levels))


def vmem(count):
    return [pl.BlockSpec(memory_space=pltpu.VMEM)] * count


def on_device(
    mesh, initial_temp, land_mask, pert_table, pert_index, base_kh, member_mix, base_mix, owner,
    column, interp_w, obs_inv_var, observed,
):
    mem_count, lat_count, lon_count = (mesh.shape[a] for a in ("mem", "lat", "lon"))
    owners, world = lat_count * lon_count, mem_count * lat_count * lon_count
    levels, width, length = initial_temp.shape
    local = member_mix.shape[0]
    runs, records = local + 1, owner.shape[0]
    rows = up(levels + 1, 16)
    capacity = max(2, 2 * records // owners)
    slots = up(capacity, 16 * mem_count)
    each = slots // mem_count
    offsets, ring = offsets_of(lon_count, width)
    columns = len(offsets) * width
    plans, blocks = lat_blocks(columns, ring, length)
    total = len(plans)
    own = width * length
    limit = pltpu.CompilerParams(vmem_limit_bytes=48 << 20)

    cells = jnp.concatenate(
        [
            initial_temp.astype(BF),
            land_mask.astype(BF)[None],
            jnp.zeros((rows - levels - 1, width, length), BF),
        ],
        0,
    )
    edge = jnp.concatenate([cells[:, :, length - SIDE :], cells[:, :, :SIDE]], 2)
    edge = edge.reshape(rows, width * CELL)
    edge = jnp.pad(edge, ((0, 0), (0, 128 - width * CELL)))
    main = cells.reshape(rows, own)

    dma = pltpu.SemaphoreType.DMA
    near_count = max(1, len(offsets) - 1)
    near, halo, ids = pl.pallas_call(
        functools.partial(exchange_kernel, (lat_count, lon_count, offsets, slots)),
        out_shape=(
            jax.ShapeDtypeStruct((near_count, rows, own), BF),
            jax.ShapeDtypeStruct((len(offsets), 2, rows, 128), BF),
            jax.ShapeDtypeStruct((owners, 8, records), F32),
        ),
        in_specs=vmem(4),
        out_specs=tuple(vmem(3)),
        scratch_shapes=[
            dma((near_count,)), dma((near_count,)),
            dma((len(offsets), 2)), dma((len(offsets), 2)),
            dma((owners - 1,)), dma((owners - 1,)),
        ],
        compiler_params=pltpu.CompilerParams(
            collective_id=0, has_side_effects=True, vmem_limit_bytes=48 << 20
        ),
    )(main, edge, owner.reshape(1, records), column.reshape(1, records))

    fields, picks, base = pl.pallas_call(
        functools.partial(
            steps_kernel, (lat_count, lon_count, offsets, ring, slots, mem_count), plans
        ),
        out_shape=(
            jax.ShapeDtypeStruct((runs, rows, own), BF),
            jax.ShapeDtypeStruct((owners, mem_count, local, each, 128), BF),
            jax.ShapeDtypeStruct((owners, slots, 128), BF),
        ),
        in_specs=[pl.BlockSpec(memory_space=pltpu.SMEM)] + vmem(9),
        out_specs=tuple(vmem(3)),
        scratch_shapes=[
            pltpu.VMEM((runs * rows, total * 128), BF),
            pltpu.VMEM((runs * rows, total * 128), BF),
            pltpu.VMEM((runs * 128, own), BF),
        ],
        compiler_params=limit,
    )(
        pert_index, main, near, halo, ids, jnp.asarray(blocks, BF), pert_table,
        base_kh.reshape(1, levels), member_mix, base_mix,
    )

    sums, misfit = pl.pallas_call(
        functools.partial(gram_kernel, (mem_count, lat_count, lon_count, slots)),
        out_shape=(
            jax.ShapeDtypeStruct((local * mem_count, 128), F32),
            jax.ShapeDtypeStruct((records, levels), F32),
        ),
        in_specs=vmem(7),
        out_specs=tuple(vmem(2)),
        scratch_shapes=[
            pltpu.VMEM((world, local, each, 128), BF),
            pltpu.VMEM((owners, slots, 128), BF),
            pltpu.VMEM((world, local * mem_count, 128), F32),
            dma((world - 1,)), dma((world - 1,)),
            dma((owners - 1,)), dma((owners - 1,)),
            dma((world - 1,)), dma((world - 1,)),
        ],
        compiler_params=pltpu.CompilerParams(
            collective_id=1, has_side_effects=True, vmem_limit_bytes=48 << 20
        ),
    )(picks, base, ids, owner, interp_w, obs_inv_var, observed)

    members = local * mem_count
    final = fields[:, :levels].reshape(runs, levels, width, length)
    return (final[:local], final[local], sums[:, :members], sums[:, members], misfit)


def solution(mesh):
    placed = (
        P(None, "lon", "lat"),
        P("lon", "lat"),
        P(),
        P("mem"),
        P(),
        P("mem", None, None),
        P(),
        P(("lat", "lon"), None),
        P(("lat", "lon")),
        P(("lat", "lon"), None),
        P(("lat", "lon"), None),
        P(("lat", "lon"), None),
    )
    return jax.shard_map(
        functools.partial(on_device, mesh),
        mesh=mesh,
        in_specs=placed,
        out_specs=(
            P("mem", None, "lon", "lat"),
            P(None, "lon", "lat"),
            P(),
            P(),
            P(("lat", "lon"), None),
        ),
        check_vma=False,
    )
```

```python
import functools

import jax
import jax.numpy as jnp
import numpy as np
from jax import lax
from jax.experimental import pallas as pl
from jax.experimental.pallas import tpu as pltpu
from jax.sharding import PartitionSpec as P

STEPS = 5
SIDE = 8
CELL = 2 * SIDE
MESH = pl.DeviceIdType.MESH
BF, F32, I32 = jnp.bfloat16, jnp.float32, jnp.int32


def up(value, multiple):
    return -(-value // multiple) * multiple


def offsets_of(lon_count, width):
    reach = -(-STEPS // width)
    if 2 * reach + 1 >= lon_count:
        return list(range(lon_count)), True
    return list(range(-reach, reach + 1)), False


def lat_blocks(columns, ring, length):
    per = 128 // CELL
    halo_tiles = -(-columns // per)
    total = columns + halo_tiles

    def where(col, lat):
        if 0 <= lat < length:
            return col * length + lat
        inside = lat + SIDE if lat < 0 else lat - length + SIDE
        return (columns + col // per) * 128 + (col % per) * CELL + inside

    matrix = {}

    def put(source, target, amount):
        key = (source // 128, target // 128)
        block = matrix.setdefault(key, np.zeros((128, 128), np.float32))
        block[source % 128, target % 128] += amount

    for col in range(columns):
        for lat in range(-SIDE, length + SIDE):
            target = where(col, lat)
            put(target, target, -4.0)
            for step in (-1, 1):
                if -SIDE <= lat + step < length + SIDE:
                    put(where(col, lat + step), target, 1.0)
                near = col + step
                if ring:
                    near %= columns
                if 0 <= near < columns and not 0 <= lat < length:
                    put(where(near, lat), target, 1.0)
    plans, stacked = [], []
    for tile in range(total):
        sources = [s for s in range(total) if (s, tile) in matrix]
        start = sum(b.shape[0] for b in stacked)
        stacked += [matrix[(s, tile)] for s in sources]
        plans.append((sources, start))
    return plans, np.concatenate(stacked, 0)


def group_of(axis_sizes):
    lat_count, lon_count = axis_sizes
    me = lax.axis_index("lat") * lon_count + lax.axis_index("lon")
    return me, lambda ll: {"lat": ll // lon_count, "lon": ll % lon_count}


def exchange_kernel(
    sizes, field_ref, mask_ref, owner_ref, column_ref, w_ref, inv_ref, obs_ref,
    main_ref, near_ref, halo_ref, got_ref, stage_ref, edge_ref, message_ref,
    main_send, main_recv, halo_send, halo_recv, got_send, got_recv,
):
    lat_count, lon_count, offsets, slots, each = sizes
    owners = lat_count * lon_count
    lat, lon, mem = lax.axis_index("lat"), lax.axis_index("lon"), lax.axis_index("mem")
    me, place = group_of((lat_count, lon_count))
    barrier = pltpu.get_barrier_semaphore()

    def greet(d, carry):
        pl.semaphore_signal(
            barrier, inc=1, device_id=place((me + d) % owners), device_id_type=MESH
        )
        return carry

    lax.fori_loop(1, owners, greet, 0)

    levels, width, length = field_ref.shape
    rows = main_ref.shape[0]
    stage_ref[levels // 8 * 8 :, :] = jnp.zeros((rows - levels // 8 * 8, width * length), F32)
    lane = lax.broadcasted_iota(I32, (1, 128), 1)
    for c in range(width):
        stage_ref[:levels, c * length : (c + 1) * length] = field_ref[:, c, :]
        stage_ref[levels : levels + 1, c * length : (c + 1) * length] = mask_ref[
            c : c + 1, :
        ].astype(F32)
    edge = jnp.zeros((rows, 128), F32)
    for c in range(width):
        cells = stage_ref[:, c * length : (c + 1) * length]
        main_ref[:, c * length : (c + 1) * length] = cells.astype(BF)
        edge = jnp.where(lane // CELL == c, pltpu.roll(cells, c * CELL + SIDE, 1), edge)
    edge_ref[...] = edge.astype(BF)

    records = owner_ref.shape[1]
    target = owner_ref[...]
    match = (lax.broadcasted_iota(I32, (up(owners, 16), records), 0) == target).astype(BF)
    before = (
        lax.broadcasted_iota(I32, (records, records), 0)
        < lax.broadcasted_iota(I32, (records, records), 1)
    ).astype(BF)
    earlier = jnp.dot(match, before, preferred_element_type=F32)
    rank = jnp.sum(earlier * match.astype(F32), axis=0, keepdims=True)
    position = target.astype(F32) * slots + rank
    cell = column_ref[...].astype(F32) + 1.0
    pl.semaphore_wait(barrier, owners - 1)

    copies = []
    near = 0
    for index, offset in enumerate(offsets):
        to_lon = (lon - offset + lon_count) % lon_count
        if offset != 0:
            copies.append(
                pltpu.make_async_remote_copy(
                    main_ref, near_ref.at[near], main_send.at[near], main_recv.at[near],
                    device_id={"lat": lat, "lon": to_lon}, device_id_type=MESH,
                )
            )
            near += 1
        for side, step in ((0, 1), (1, lat_count - 1)):
            copies.append(
                pltpu.make_async_remote_copy(
                    edge_ref, halo_ref.at[index, side],
                    halo_send.at[index, side], halo_recv.at[index, side],
                    device_id={"lat": (lat + step) % lat_count, "lon": to_lon},
                    device_id_type=MESH,
                )
            )
    for copy in copies:
        copy.start()

    message_ref[...] = jnp.zeros_like(message_ref)
    slot = (
        lax.broadcasted_iota(I32, (owners, each, records), 0) * slots
        + lax.broadcasted_iota(I32, (owners, each, records), 1)
        + mem * each
    ).reshape(owners * each, records)
    hot = jnp.where(slot.astype(F32) == position, 1.0, 0.0)
    for kind, ref in enumerate((w_ref, inv_ref, obs_ref)):
        chosen = lax.dot_general(
            hot, ref[...], (((1,), (1,)), ((), ())),
            precision=lax.Precision.HIGHEST, preferred_element_type=F32,
        )
        message_ref[:, kind * each : (kind + 1) * each, :levels] = chosen.reshape(
            owners, each, levels
        )
    lines = records // 128
    row = lax.broadcasted_iota(I32, (8, 128), 0)
    head = jnp.zeros((8, 128), F32)
    for line in range(lines):
        part = slice(line * 128, (line + 1) * 128)
        head = jnp.where(row == line, position[:, part], head)
        head = jnp.where(row == lines + line, cell[:, part], head)
    message_ref[:, 3 * each :, :] = jnp.broadcast_to(head[None], (owners, 8, 128))
    got_ref[me] = message_ref[me]

    def got_copy(d, slot):
        to = (me + d) % owners
        return pltpu.make_async_remote_copy(
            message_ref.at[to], got_ref.at[slot], got_send.at[d - 1], got_recv.at[d - 1],
            device_id=place(to), device_id_type=MESH,
        )

    def send(d, carry):
        got_copy(d, me).start()
        return carry

    def wait(d, carry):
        got_copy(d, (me + owners - d) % owners).wait()
        return carry

    lax.fori_loop(1, owners, send, 0)
    lax.fori_loop(1, owners, wait, 0)
    for copy in copies:
        copy.wait()


def lines_of(known, start, records):
    lines = records // 128
    rows = [known[start + i : start + i + 1] for i in range(2 * lines)]
    return jnp.concatenate(rows[:lines], 1), jnp.concatenate(rows[lines:], 1)


def steps_kernel(
    sizes, plans, pert_index, main_ref, near_ref, halo_ref, ids_ref, blocks_ref, table_ref,
    base_kh_ref, mix_ref, base_mix_ref, fields_ref, picks_ref, base_ref, v_ref, rs_ref, f_ref,
):
    lat_count, lon_count, offsets, ring, slots, mem_count, records = sizes
    owners = lat_count * lon_count
    lat = lax.axis_index("lat")
    me = lat * lon_count + lax.axis_index("lon")
    rows = main_ref.shape[0]
    levels = table_ref.shape[1]
    own = main_ref.shape[1]
    runs = mix_ref.shape[0] + 1
    columns = len(offsets) * (own // 128)
    total = len(plans)
    first = offsets.index(0) * own
    lane = lax.broadcasted_iota(I32, (1, 128), 1)

    near = 0
    for index, offset in enumerate(offsets):
        if offset == 0:
            block = main_ref[...]
        else:
            block = near_ref[near]
            near += 1
        for run in range(runs):
            v_ref[run * rows : (run + 1) * rows, index * own : (index + 1) * own] = block
    low = lane % CELL < SIDE
    lanes = own // 128 * CELL
    per = 128 // lanes
    for tile in range(total - columns):
        value = jnp.zeros((rows, 128), F32)
        for part in range(per):
            index = tile * per + part
            if index >= len(offsets):
                continue
            prior = jnp.where(lat > 0, halo_ref[index, 0].astype(F32), 0.0)
            later = jnp.where(lat < lat_count - 1, halo_ref[index, 1].astype(F32), 0.0)
            both = jnp.where(low, prior, later)
            if part:
                both = pltpu.roll(both, part * lanes, 1)
            value = jnp.where((lane >= part * lanes) & (lane < (part + 1) * lanes), both, value)
        at = (columns + tile) * 128
        for run in range(runs):
            v_ref[run * rows : (run + 1) * rows, at : at + 128] = value.astype(BF)

    tail = v_ref[levels // 16 * 16 : levels // 16 * 16 + 16, :].astype(F32)
    open_row = tail[levels % 16 : levels % 16 + 1, :]

    def column_of(row):
        eye = lax.broadcasted_iota(I32, (rows, levels), 0) == lax.broadcasted_iota(
            I32, (rows, levels), 1
        )
        return jnp.sum(jnp.where(eye, row, 0.0), axis=1, keepdims=True)

    kh = [column_of(table_ref[pl.ds(pert_index[r], 1), :]) for r in range(runs - 1)]
    kh = jnp.concatenate(kh + [column_of(base_kh_ref[...])], 0)
    at_start = jnp.where(lat == 0, 1.0, 0.0)
    at_end = jnp.where(lat == lat_count - 1, 1.0, 0.0)
    edge = jnp.where(lane == 0, at_start, 0.0) + jnp.where(lane == 127, at_end, 0.0)

    def step(number, carry):
        for tile in range(total):
            sources, start = plans[tile]
            left = jnp.concatenate([v_ref[:, s * 128 : (s + 1) * 128] for s in sources], 1)
            right = blocks_ref[start : start + 128 * len(sources), :]
            laplace = jnp.dot(left, right, preferred_element_type=F32)
            values = v_ref[:, tile * 128 : (tile + 1) * 128].astype(F32)
            if tile < columns:
                for shift in (-1, 1):
                    other = tile + shift
                    if ring:
                        other %= columns
                    if 0 <= other < columns:
                        laplace += v_ref[:, other * 128 : (other + 1) * 128].astype(F32)
                laplace += edge * values
            rs_ref[:, tile * 128 : (tile + 1) * 128] = (values + kh * laplace).astype(BF)
        for run in range(runs):
            mix = mix_ref[run] if run < runs - 1 else base_mix_ref[...]
            top = run * rows
            for start in range(0, total, 3):
                end = min(start + 3, total)
                part = slice(start * 128, end * 128)
                right_side = rs_ref[top : top + levels, part]
                vertical = right_side.astype(F32) + jnp.dot(
                    mix, right_side, preferred_element_type=F32
                )
                values = v_ref[top : top + levels, part].astype(F32)
                v_ref[top : top + levels, part] = jnp.where(
                    open_row[:, part] > 0.5, vertical, values
                ).astype(BF)
        return carry

    lax.fori_loop(0, STEPS, step, 0)

    f_ref[...] = jnp.zeros_like(f_ref)
    for run in range(runs):
        block = v_ref[run * rows : (run + 1) * rows, first : first + own]
        fields_ref[run] = block
        f_ref[run * 128 : run * 128 + rows, :] = block

    each = slots // mem_count
    fields = f_ref[...]

    def pick(source, carry):
        position, column = lines_of(ids_ref[source], 3 * each, records)
        slot = lax.broadcasted_iota(I32, (slots, records), 0) + me * slots
        chosen = jnp.where(slot.astype(F32) == position, column, 0.0)
        cell = jnp.sum(chosen, axis=1, keepdims=True) - 1.0
        lanes_own = lax.broadcasted_iota(I32, (slots, own), 1).astype(F32)
        hot = jnp.where(lanes_own == cell, 1.0, 0.0).astype(BF)
        got = lax.dot_general(
            hot, fields, (((1,), (1,)), ((), ())), preferred_element_type=F32
        ).astype(BF)
        for run in range(runs - 1):
            for j in range(mem_count):
                picks_ref[j, source, run] = got[
                    j * each : (j + 1) * each, run * 128 : (run + 1) * 128
                ]
        base_ref[source] = got[:, (runs - 1) * 128 :]
        return carry

    lax.fori_loop(0, owners, pick, 0)


def gram_kernel(
    sizes, picks_ref, base_ref, message_ref, w_ref, obs_ref, sum_ref, misfit_ref,
    got_ref, base_got, near_ref, tiles_ref, got_send, got_recv, base_send, base_recv,
    near_send, near_recv, sum_send, sum_recv,
):
    mem_count, lat_count, lon_count, slots = sizes
    owners = lat_count * lon_count
    mem = lax.axis_index("mem")
    plane, place = group_of((lat_count, lon_count))
    barrier = pltpu.get_barrier_semaphore()
    levels, records = w_ref.shape
    each = slots // mem_count
    local = picks_ref.shape[2]
    members = local * mem_count

    def greet(d, carry):
        pl.semaphore_signal(
            barrier, inc=1, device_id=place((plane + d) % owners), device_id_type=MESH
        )
        return carry

    for d in range(1, mem_count):
        pl.semaphore_signal(
            barrier, inc=1, device_id={"mem": (mem + d) % mem_count}, device_id_type=MESH
        )
    lax.fori_loop(1, owners, greet, 0)
    got_ref[mem] = picks_ref[mem]
    base_got[plane] = base_ref[plane]
    pl.semaphore_wait(barrier, owners - 1 + mem_count - 1)

    def mem_copy(d, source, target, send, recv):
        return pltpu.make_async_remote_copy(
            source, target, send.at[d - 1], recv.at[d - 1],
            device_id={"mem": (mem + d) % mem_count}, device_id_type=MESH,
        )

    def plane_copy(d, source, target, send, recv):
        return pltpu.make_async_remote_copy(
            source, target, send.at[d - 1], recv.at[d - 1],
            device_id=place((plane + d) % owners), device_id_type=MESH,
        )

    def got_copy(d, slot):
        to = (mem + d) % mem_count
        return mem_copy(d, picks_ref.at[to], got_ref.at[slot], got_send, got_recv)

    def base_copy(d, slot):
        to = (plane + d) % owners
        return plane_copy(d, base_ref.at[to], base_got.at[slot], base_send, base_recv)

    for d in range(1, mem_count):
        got_copy(d, mem).start()

    def start_base(d, carry):
        base_copy(d, plane).start()
        return carry

    lax.fori_loop(1, owners, start_base, 0)

    group = 8 if owners % 8 == 0 else owners
    wide = group * each
    lane = lax.broadcasted_iota(I32, (1, 128), 1)

    def interpolated(value, weight):
        deeper = jnp.where(lane == levels - 1, value, pltpu.roll(value, 127, 1))
        return weight * value + (1.0 - weight) * deeper

    for d in range(1, mem_count):
        got_copy(d, (mem + mem_count - d) % mem_count).wait()

    def gram(chunk, total):
        at = pl.ds(chunk * group, group)
        weight, inv_var, measured = (
            message_ref[at, kind * each : (kind + 1) * each, :].reshape(wide, 128)
            for kind in range(3)
        )
        base = base_ref[at, pl.ds(pl.multiple_of(mem * each, each), each)]
        base = interpolated(base.reshape(wide, 128).astype(F32), weight)
        others = []
        for m in range(members):
            cells = got_ref[m // local, at, m % local].reshape(wide, 128).astype(F32)
            green = interpolated(cells, weight) - base
            others.append(green.astype(BF).astype(F32))
        others.append(measured - base)
        lines = []
        for m in range(members):
            weighted = others[m] * inv_var
            for n in range(members + 1):
                if n < m:
                    lines.append(lines[n * 16 + m])
                else:
                    lines.append(jnp.sum(weighted * others[n], axis=0, keepdims=True))
            lines += [jnp.zeros((1, 128), F32)] * (16 - members - 1)
        return total + jnp.concatenate(lines, 0)

    total = jnp.zeros((members * 16, 128), F32)
    if owners == group:
        total = gram(0, total)
    else:
        total = lax.fori_loop(0, owners // group, gram, total)
    sums = jnp.sum(total, axis=1, keepdims=True)
    spot = lax.broadcasted_iota(I32, (members, 16, 128), 1) == lax.broadcasted_iota(
        I32, (members, 16, 128), 2
    )
    near_ref[mem] = jnp.sum(jnp.where(spot, sums.reshape(members, 16, 1), 0.0), axis=1)

    def near_copy(d, slot):
        return mem_copy(d, near_ref.at[mem], near_ref.at[slot], near_send, near_recv)

    for d in range(1, mem_count):
        near_copy(d, mem).start()

    def wait_base(d, carry):
        base_copy(d, (plane + owners - d) % owners).wait()
        return carry

    lax.fori_loop(1, owners, wait_base, 0)
    position, _ = lines_of(message_ref[plane], 3 * each, records)

    def spread(chunk, total):
        cells = base_got[pl.ds(chunk * group, group)].reshape(group * slots, 128)
        at = lax.broadcasted_iota(I32, (group * slots, records), 0) + chunk * (group * slots)
        hot = jnp.where(at.astype(F32) == position, 1.0, 0.0).astype(BF)
        return total + lax.dot_general(
            cells, hot, (((0,), (0,)), ((), ())), preferred_element_type=F32
        )

    def misfit():
        picked = jnp.zeros((128, records), F32)
        if owners == group:
            picked = spread(0, picked)
        else:
            picked = lax.fori_loop(0, owners // group, spread, picked)
        deeper = pltpu.roll(picked, 127, 0)
        level = lax.broadcasted_iota(I32, (128, 1), 0)
        deeper = jnp.where(level == levels - 1, picked, deeper)
        weight = w_ref[...]
        misfit_ref[...] = obs_ref[...] - (
            weight * picked[:levels] + (1.0 - weight) * deeper[:levels]
        )

    for d in range(1, mem_count):
        near_copy(d, mem).wait_send()
        near_copy(d, (mem + mem_count - d) % mem_count).wait_recv()
    tiles_ref[plane] = jnp.sum(near_ref[...], axis=0)

    def sum_copy(d, slot):
        return plane_copy(d, tiles_ref.at[plane], tiles_ref.at[slot], sum_send, sum_recv)

    def start_sum(d, carry):
        sum_copy(d, plane).start()
        return carry

    def wait_sum(d, carry):
        sum_copy(d, plane).wait_send()
        sum_copy(d, (plane + owners - d) % owners).wait_recv()
        return carry

    lax.fori_loop(1, owners, start_sum, 0)
    misfit()
    lax.fori_loop(1, owners, wait_sum, 0)
    sum_ref[...] = jnp.sum(tiles_ref[...], axis=0) * (1.0 / (records * owners * levels))


def vmem(count):
    return [pl.BlockSpec(memory_space=pltpu.VMEM)] * count


def on_device(
    mesh, initial_temp, land_mask, pert_table, pert_index, base_kh, member_mix, base_mix, owner,
    column, interp_w, obs_inv_var, observed,
):
    mem_count, lat_count, lon_count = (mesh.shape[a] for a in ("mem", "lat", "lon"))
    owners = lat_count * lon_count
    levels, width, length = initial_temp.shape
    local = member_mix.shape[0]
    runs, records = local + 1, owner.shape[0]
    rows = up(levels + 1, 16)
    capacity = max(2, 2 * records // owners)
    slots = up(capacity, 16 * mem_count)
    each = slots // mem_count
    offsets, ring = offsets_of(lon_count, width)
    columns = len(offsets) * width
    plans, blocks = lat_blocks(columns, ring, length)
    total = len(plans)
    own = width * length
    limit = pltpu.CompilerParams(vmem_limit_bytes=48 << 20)

    w, inv_var, measured = interp_w.T, obs_inv_var.T, observed.T
    dma = pltpu.SemaphoreType.DMA
    near_count = max(1, len(offsets) - 1)
    main, near, halo, messages = pl.pallas_call(
        functools.partial(exchange_kernel, (lat_count, lon_count, offsets, slots, each)),
        out_shape=(
            jax.ShapeDtypeStruct((rows, own), BF),
            jax.ShapeDtypeStruct((near_count, rows, own), BF),
            jax.ShapeDtypeStruct((len(offsets), 2, rows, 128), BF),
            jax.ShapeDtypeStruct((owners, 3 * each + 8, 128), F32),
        ),
        in_specs=vmem(7),
        out_specs=tuple(vmem(4)),
        scratch_shapes=[
            pltpu.VMEM((rows, own), F32),
            pltpu.VMEM((rows, 128), BF),
            pltpu.VMEM((owners, 3 * each + 8, 128), F32),
            dma((near_count,)), dma((near_count,)),
            dma((len(offsets), 2)), dma((len(offsets), 2)),
            dma((owners - 1,)), dma((owners - 1,)),
        ],
        compiler_params=pltpu.CompilerParams(
            collective_id=0, has_side_effects=True, vmem_limit_bytes=48 << 20
        ),
    )(
        initial_temp, land_mask, owner.reshape(1, records), column.reshape(1, records),
        w, inv_var, measured,
    )

    fields, picks, base = pl.pallas_call(
        functools.partial(
            steps_kernel, (lat_count, lon_count, offsets, ring, slots, mem_count, records), plans
        ),
        out_shape=(
            jax.ShapeDtypeStruct((runs, rows, own), BF),
            jax.ShapeDtypeStruct((mem_count, owners, local, each, 128), BF),
            jax.ShapeDtypeStruct((owners, slots, 128), BF),
        ),
        in_specs=[pl.BlockSpec(memory_space=pltpu.SMEM)] + vmem(9),
        out_specs=tuple(vmem(3)),
        scratch_shapes=[
            pltpu.VMEM((runs * rows, total * 128), BF),
            pltpu.VMEM((runs * rows, total * 128), BF),
            pltpu.VMEM((runs * 128, own), BF),
        ],
        compiler_params=limit,
    )(
        pert_index, main, near, halo, messages, jnp.asarray(blocks, BF), pert_table,
        base_kh.reshape(1, levels), member_mix, base_mix,
    )

    sums, misfit = pl.pallas_call(
        functools.partial(gram_kernel, (mem_count, lat_count, lon_count, slots)),
        out_shape=(
            jax.ShapeDtypeStruct((local * mem_count, 128), F32),
            jax.ShapeDtypeStruct((levels, records), F32),
        ),
        in_specs=vmem(5),
        out_specs=tuple(vmem(2)),
        scratch_shapes=[
            pltpu.VMEM((mem_count, owners, local, each, 128), BF),
            pltpu.VMEM((owners, slots, 128), BF),
            pltpu.VMEM((mem_count, local * mem_count, 128), F32),
            pltpu.VMEM((owners, local * mem_count, 128), F32),
            dma((mem_count - 1,)), dma((mem_count - 1,)),
            dma((owners - 1,)), dma((owners - 1,)),
            dma((mem_count - 1,)), dma((mem_count - 1,)),
            dma((owners - 1,)), dma((owners - 1,)),
        ],
        compiler_params=pltpu.CompilerParams(
            collective_id=1, has_side_effects=True, vmem_limit_bytes=48 << 20
        ),
    )(picks, base, messages, w, measured)

    members = local * mem_count
    final = fields[:, :levels].reshape(runs, levels, width, length)
    return (final[:local], final[local], sums[:, :members], sums[:, members], misfit.T)


def solution(mesh):
    placed = (
        P(None, "lon", "lat"),
        P("lon", "lat"),
        P(),
        P("mem"),
        P(),
        P("mem", None, None),
        P(),
        P(("lat", "lon"), None),
        P(("lat", "lon")),
        P(("lat", "lon"), None),
        P(("lat", "lon"), None),
        P(("lat", "lon"), None),
    )
    return jax.shard_map(
        functools.partial(on_device, mesh),
        mesh=mesh,
        in_specs=placed,
        out_specs=(
            P("mem", None, "lon", "lat"),
            P(None, "lon", "lat"),
            P(),
            P(),
            P(("lat", "lon"), None),
        ),
        check_vma=False,
    )
```

```python
import functools

import jax
import jax.numpy as jnp
import numpy as np
from jax import lax
from jax.experimental import pallas as pl
from jax.experimental.pallas import tpu as pltpu
from jax.sharding import PartitionSpec as P

STEPS = 5
SIDE = 8
CELL = 2 * SIDE
MESH = pl.DeviceIdType.MESH
BF, F32, I32 = jnp.bfloat16, jnp.float32, jnp.int32


def up(value, multiple):
    return -(-value // multiple) * multiple


def offsets_of(lon_count, width):
    reach = -(-STEPS // width)
    if 2 * reach + 1 >= lon_count:
        return list(range(lon_count)), True
    return list(range(-reach, reach + 1)), False


def lat_blocks(columns, ring, length):
    per = 128 // CELL
    halo_tiles = -(-columns // per)
    total = columns + halo_tiles

    def where(col, lat):
        if 0 <= lat < length:
            return col * length + lat
        inside = lat + SIDE if lat < 0 else lat - length + SIDE
        return (columns + col // per) * 128 + (col % per) * CELL + inside

    matrix = {}

    def put(source, target, amount):
        key = (source // 128, target // 128)
        block = matrix.setdefault(key, np.zeros((128, 128), np.float32))
        block[source % 128, target % 128] += amount

    for col in range(columns):
        for lat in range(-SIDE, length + SIDE):
            target = where(col, lat)
            put(target, target, -4.0)
            for step in (-1, 1):
                if -SIDE <= lat + step < length + SIDE:
                    put(where(col, lat + step), target, 1.0)
                near = col + step
                if ring:
                    near %= columns
                if 0 <= near < columns and not 0 <= lat < length:
                    put(where(near, lat), target, 1.0)
    plans, stacked = [], []
    for tile in range(total):
        sources = [s for s in range(total) if (s, tile) in matrix]
        start = sum(b.shape[0] for b in stacked)
        stacked += [matrix[(s, tile)] for s in sources]
        plans.append((sources, start))
    return plans, np.concatenate(stacked, 0)


def group_of(axis_sizes):
    lat_count, lon_count = axis_sizes
    me = lax.axis_index("lat") * lon_count + lax.axis_index("lon")
    return me, lambda ll: {"lat": ll // lon_count, "lon": ll % lon_count}


def exchange_kernel(
    sizes, *refs
):
    sources, refs = refs[:7], refs[7:]
    main_ref, near_ref, halo_ref, got_ref, stage_ref, edge_ref, message_ref = refs[:7]
    fetched, fetch_sem = refs[7:14], refs[14]
    field_ref, mask_ref, owner_ref, column_ref, w_ref, inv_ref, obs_ref = fetched
    exchange(sizes, sources, fetched, fetch_sem, field_ref, mask_ref, owner_ref, column_ref,
        w_ref, inv_ref, obs_ref, main_ref, near_ref, halo_ref, got_ref, stage_ref, edge_ref,
        message_ref, *refs[15:])


def exchange(
    sizes, sources, fetched, fetch_sem, field_ref, mask_ref, owner_ref, column_ref,
    w_ref, inv_ref, obs_ref, main_ref, near_ref, halo_ref, got_ref, stage_ref, edge_ref,
    message_ref, main_send, main_recv, halo_send, halo_recv, got_send, got_recv,
):
    lat_count, lon_count, offsets, slots, each = sizes
    owners = lat_count * lon_count
    lat, lon, mem = lax.axis_index("lat"), lax.axis_index("lon"), lax.axis_index("mem")
    me, place = group_of((lat_count, lon_count))
    barrier = pltpu.get_barrier_semaphore()
    fetches = [
        pltpu.make_async_copy(source, target, fetch_sem.at[i])
        for i, (source, target) in enumerate(zip(sources, fetched))
    ]
    for fetch in fetches:
        fetch.start()

    def greet(d, carry):
        pl.semaphore_signal(
            barrier, inc=1, device_id=place((me + d) % owners), device_id_type=MESH
        )
        return carry

    lax.fori_loop(1, owners, greet, 0)

    levels, width, length = field_ref.shape
    rows = main_ref.shape[0]
    stage_ref[levels // 8 * 8 :, :] = jnp.zeros((rows - levels // 8 * 8, width * length), F32)
    lane = lax.broadcasted_iota(I32, (1, 128), 1)
    for fetch in fetches[:4]:
        fetch.wait()
    for c in range(width):
        stage_ref[:levels, c * length : (c + 1) * length] = field_ref[:, c, :]
        stage_ref[levels : levels + 1, c * length : (c + 1) * length] = mask_ref[
            c : c + 1, :
        ].astype(F32)
    edge = jnp.zeros((rows, 128), F32)
    for c in range(width):
        cells = stage_ref[:, c * length : (c + 1) * length]
        main_ref[:, c * length : (c + 1) * length] = cells.astype(BF)
        edge = jnp.where(lane // CELL == c, pltpu.roll(cells, c * CELL + SIDE, 1), edge)
    edge_ref[...] = edge.astype(BF)

    records = owner_ref.shape[1]
    target = owner_ref[...]
    match = (lax.broadcasted_iota(I32, (up(owners, 16), records), 0) == target).astype(BF)
    before = (
        lax.broadcasted_iota(I32, (records, records), 0)
        < lax.broadcasted_iota(I32, (records, records), 1)
    ).astype(BF)
    earlier = jnp.dot(match, before, preferred_element_type=F32)
    rank = jnp.sum(earlier * match.astype(F32), axis=0, keepdims=True)
    position = target.astype(F32) * slots + rank
    spot, cell = position.astype(I32), column_ref[...] + 1
    digits = [(n >> 6, n & 63) for n in (spot, cell)]
    digits = [d.astype(F32) for pair in digits for d in pair]
    pl.semaphore_wait(barrier, owners - 1)

    copies = []
    near = 0
    for index, offset in enumerate(offsets):
        to_lon = (lon - offset + lon_count) % lon_count
        if offset != 0:
            copies.append(
                pltpu.make_async_remote_copy(
                    main_ref, near_ref.at[near], main_send.at[near], main_recv.at[near],
                    device_id={"lat": lat, "lon": to_lon}, device_id_type=MESH,
                )
            )
            near += 1
        for side, step in ((0, 1), (1, lat_count - 1)):
            copies.append(
                pltpu.make_async_remote_copy(
                    edge_ref, halo_ref.at[index, side],
                    halo_send.at[index, side], halo_recv.at[index, side],
                    device_id={"lat": (lat + step) % lat_count, "lon": to_lon},
                    device_id_type=MESH,
                )
            )
    for copy in copies:
        copy.start()

    message_ref[...] = jnp.zeros_like(message_ref)
    for fetch in fetches[4:]:
        fetch.wait()
    slot = (
        lax.broadcasted_iota(I32, (owners, each, records), 0) * slots
        + lax.broadcasted_iota(I32, (owners, each, records), 1)
        + mem * each
    ).reshape(owners * each, records)
    hot = jnp.where(slot.astype(F32) == position, 1.0, 0.0)
    for kind, ref in enumerate((w_ref, inv_ref, obs_ref)):
        chosen = lax.dot_general(
            hot, ref[...], (((1,), (1,)), ((), ())),
            precision=lax.Precision.HIGHEST, preferred_element_type=F32,
        )
        message_ref[:, kind * each : (kind + 1) * each, :levels] = chosen.reshape(
            owners, each, levels
        ).astype(BF)
    lines = records // 128
    row = lax.broadcasted_iota(I32, (16, 128), 0)
    head = jnp.zeros((16, 128), F32)
    for line in range(lines):
        part = slice(line * 128, (line + 1) * 128)
        for kind, digit in enumerate(digits):
            head = jnp.where(row == kind * lines + line, digit[:, part], head)
    message_ref[:, 3 * each :, :] = jnp.broadcast_to(head.astype(BF)[None], (owners, 16, 128))
    got_ref[me] = message_ref[me]

    def got_copy(d, slot):
        to = (me + d) % owners
        return pltpu.make_async_remote_copy(
            message_ref.at[to], got_ref.at[slot], got_send.at[d - 1], got_recv.at[d - 1],
            device_id=place(to), device_id_type=MESH,
        )

    def send(d, carry):
        got_copy(d, me).start()
        return carry

    def wait(d, carry):
        got_copy(d, (me + owners - d) % owners).wait()
        return carry

    lax.fori_loop(1, owners, send, 0)
    lax.fori_loop(1, owners, wait, 0)
    for copy in copies:
        copy.wait()


def lines_of(known, records):
    lines = records // 128
    digits = known.astype(F32)
    rows = [digits[i : i + 1] for i in range(4 * lines)]
    high, low, cell_high, cell_low = (
        jnp.concatenate(rows[k * lines : (k + 1) * lines], 1) for k in range(4)
    )
    return high * 64.0 + low, cell_high * 64.0 + cell_low


def steps_kernel(
    sizes, plans, pert_index, main_ref, near_ref, halo_ref, ids_ref, mix_ref, base_mix_ref,
    blocks_at, table_at, base_kh_at, members_out, base_out, picks_ref, base_ref, v_ref, rs_ref,
    f_ref, blocks_ref, table_ref, base_kh_ref, wide_ref, final_ref, fetch_sem,
    out_sem,
):
    fetches = [
        pltpu.make_async_copy(source, target, fetch_sem.at[i])
        for i, (source, target) in enumerate(
            ((blocks_at, blocks_ref), (table_at, table_ref), (base_kh_at, base_kh_ref))
        )
    ]
    for fetch in fetches:
        fetch.start()
    lat_count, lon_count, offsets, ring, slots, mem_count, records = sizes
    owners = lat_count * lon_count
    lat = lax.axis_index("lat")
    me = lat * lon_count + lax.axis_index("lon")
    rows = main_ref.shape[0]
    levels = table_ref.shape[1]
    own = main_ref.shape[1]
    runs = mix_ref.shape[0] + 1
    columns = len(offsets) * (own // 128)
    total = len(plans)
    first = offsets.index(0) * own
    lane = lax.broadcasted_iota(I32, (1, 128), 1)

    near = 0
    for index, offset in enumerate(offsets):
        if offset == 0:
            block = main_ref[...]
        else:
            block = near_ref[near]
            near += 1
        for run in range(runs):
            v_ref[run * rows : (run + 1) * rows, index * own : (index + 1) * own] = block
    low = lane % CELL < SIDE
    lanes = own // 128 * CELL
    per = 128 // lanes
    for tile in range(total - columns):
        value = jnp.zeros((rows, 128), F32)
        for part in range(per):
            index = tile * per + part
            if index >= len(offsets):
                continue
            prior = jnp.where(lat > 0, halo_ref[index, 0].astype(F32), 0.0)
            later = jnp.where(lat < lat_count - 1, halo_ref[index, 1].astype(F32), 0.0)
            both = jnp.where(low, prior, later)
            if part:
                both = pltpu.roll(both, part * lanes, 1)
            value = jnp.where((lane >= part * lanes) & (lane < (part + 1) * lanes), both, value)
        at = (columns + tile) * 128
        for run in range(runs):
            v_ref[run * rows : (run + 1) * rows, at : at + 128] = value.astype(BF)

    tail = v_ref[levels // 16 * 16 : levels // 16 * 16 + 16, :].astype(F32)
    open_row = tail[levels % 16 : levels % 16 + 1, :]

    def column_of(row):
        eye = lax.broadcasted_iota(I32, (rows, levels), 0) == lax.broadcasted_iota(
            I32, (rows, levels), 1
        )
        return jnp.sum(jnp.where(eye, row, 0.0), axis=1, keepdims=True)

    for fetch in fetches:
        fetch.wait()
    kh = [column_of(table_ref[pl.ds(pert_index[r], 1), :]) for r in range(runs - 1)]
    kh = jnp.concatenate(kh + [column_of(base_kh_ref[...])], 0)
    at_start = jnp.where(lat == 0, 1.0, 0.0)
    at_end = jnp.where(lat == lat_count - 1, 1.0, 0.0)
    edge = jnp.where(lane == 0, at_start, 0.0) + jnp.where(lane == 127, at_end, 0.0)

    def step(number, carry):
        for tile in range(total):
            sources, start = plans[tile]
            left = jnp.concatenate([v_ref[:, s * 128 : (s + 1) * 128] for s in sources], 1)
            right = blocks_ref[start : start + 128 * len(sources), :]
            laplace = jnp.dot(left, right, preferred_element_type=F32)
            values = v_ref[:, tile * 128 : (tile + 1) * 128].astype(F32)
            if tile < columns:
                for shift in (-1, 1):
                    other = tile + shift
                    if ring:
                        other %= columns
                    if 0 <= other < columns:
                        laplace += v_ref[:, other * 128 : (other + 1) * 128].astype(F32)
                laplace += edge * values
            rs_ref[:, tile * 128 : (tile + 1) * 128] = (values + kh * laplace).astype(BF)
        for run in range(runs):
            mix = mix_ref[run] if run < runs - 1 else base_mix_ref[...]
            top = run * rows
            for start in range(0, total, 3):
                end = min(start + 3, total)
                part = slice(start * 128, end * 128)
                right_side = rs_ref[top : top + levels, part]
                vertical = right_side.astype(F32) + jnp.dot(
                    mix, right_side, preferred_element_type=F32
                )
                values = v_ref[top : top + levels, part].astype(F32)
                v_ref[top : top + levels, part] = jnp.where(
                    open_row[:, part] > 0.5, vertical, values
                ).astype(BF)
        return carry

    lax.fori_loop(0, STEPS, step, 0)

    f_ref[...] = jnp.zeros_like(f_ref)
    for run in range(runs):
        block = v_ref[run * rows : (run + 1) * rows, first : first + own]
        f_ref[run * 128 : run * 128 + rows, :] = block
        length = 128
        for c in range(own // length):
            wide_ref[run, :, c, :] = block[:levels, c * length : (c + 1) * length].astype(F32)
        final_ref[run] = wide_ref[run].astype(BF)
    outs = [
        pltpu.make_async_copy(
            final_ref.at[run], members_out.at[run] if run < runs - 1 else base_out,
            out_sem.at[run],
        )
        for run in range(runs)
    ]
    for out in outs:
        out.start()

    each = slots // mem_count
    fields = f_ref[...]

    def pick(source, carry):
        position, column = lines_of(ids_ref[source, 3 * each :], records)
        slot = lax.broadcasted_iota(I32, (slots, records), 0) + me * slots
        chosen = jnp.where(slot.astype(F32) == position, column, 0.0)
        cell = jnp.sum(chosen, axis=1, keepdims=True) - 1.0
        lanes_own = lax.broadcasted_iota(I32, (slots, own), 1).astype(F32)
        hot = jnp.where(lanes_own == cell, 1.0, 0.0).astype(BF)
        got = lax.dot_general(
            hot, fields, (((1,), (1,)), ((), ())), preferred_element_type=F32
        ).astype(BF)
        for run in range(runs - 1):
            for j in range(mem_count):
                picks_ref[j, source, run] = got[
                    j * each : (j + 1) * each, run * 128 : (run + 1) * 128
                ]
        base_ref[source] = got[:, (runs - 1) * 128 :]
        return carry

    lax.fori_loop(0, owners, pick, 0)
    for out in outs:
        out.wait()


def gram_kernel(
    sizes, picks_ref, base_ref, message_ref, w_at, obs_at, sum_ref, misfit_ref,
    w_ref, obs_ref, fetch_sem, got_ref, base_got, near_ref, tiles_ref, got_send, got_recv, base_send, base_recv,
    near_send, near_recv, sum_send, sum_recv,
):
    mem_count, lat_count, lon_count, slots = sizes
    owners = lat_count * lon_count
    mem = lax.axis_index("mem")
    plane, place = group_of((lat_count, lon_count))
    barrier = pltpu.get_barrier_semaphore()
    levels, records = w_ref.shape
    fetches = [
        pltpu.make_async_copy(w_at, w_ref, fetch_sem.at[0]),
        pltpu.make_async_copy(obs_at, obs_ref, fetch_sem.at[1]),
    ]
    for fetch in fetches:
        fetch.start()
    each = slots // mem_count
    local = picks_ref.shape[2]
    members = local * mem_count

    def greet(d, carry):
        pl.semaphore_signal(
            barrier, inc=1, device_id=place((plane + d) % owners), device_id_type=MESH
        )
        return carry

    for d in range(1, mem_count):
        pl.semaphore_signal(
            barrier, inc=1, device_id={"mem": (mem + d) % mem_count}, device_id_type=MESH
        )
    lax.fori_loop(1, owners, greet, 0)
    got_ref[mem] = picks_ref[mem]
    base_got[plane] = base_ref[plane]
    pl.semaphore_wait(barrier, owners - 1 + mem_count - 1)

    def mem_copy(d, source, target, send, recv):
        return pltpu.make_async_remote_copy(
            source, target, send.at[d - 1], recv.at[d - 1],
            device_id={"mem": (mem + d) % mem_count}, device_id_type=MESH,
        )

    def plane_copy(d, source, target, send, recv):
        return pltpu.make_async_remote_copy(
            source, target, send.at[d - 1], recv.at[d - 1],
            device_id=place((plane + d) % owners), device_id_type=MESH,
        )

    def got_copy(d, slot):
        to = (mem + d) % mem_count
        return mem_copy(d, picks_ref.at[to], got_ref.at[slot], got_send, got_recv)

    def base_copy(d, slot):
        to = (plane + d) % owners
        return plane_copy(d, base_ref.at[to], base_got.at[slot], base_send, base_recv)

    for d in range(1, mem_count):
        got_copy(d, mem).start()

    def start_base(d, carry):
        base_copy(d, plane).start()
        return carry

    lax.fori_loop(1, owners, start_base, 0)

    group = 8 if owners % 8 == 0 else owners
    wide = group * each
    lane = lax.broadcasted_iota(I32, (1, 128), 1)

    def interpolated(value, weight):
        deeper = jnp.where(lane == levels - 1, value, pltpu.roll(value, 127, 1))
        return weight * value + (1.0 - weight) * deeper

    for d in range(1, mem_count):
        got_copy(d, (mem + mem_count - d) % mem_count).wait()

    def gram(chunk, total):
        at = pl.ds(chunk * group, group)
        weight, inv_var, measured = (
            message_ref[at, kind * each : (kind + 1) * each, :].reshape(wide, 128).astype(F32)
            for kind in range(3)
        )
        base = base_ref[at, pl.ds(pl.multiple_of(mem * each, each), each)]
        base = interpolated(base.reshape(wide, 128).astype(F32), weight)
        others = []
        for m in range(members):
            cells = got_ref[m // local, at, m % local].reshape(wide, 128).astype(F32)
            green = interpolated(cells, weight) - base
            others.append(green.astype(BF).astype(F32))
        others.append(measured - base)
        lines = []
        for m in range(members):
            weighted = others[m] * inv_var
            for n in range(members + 1):
                if n < m:
                    lines.append(lines[n * 16 + m])
                else:
                    lines.append(jnp.sum(weighted * others[n], axis=0, keepdims=True))
            lines += [jnp.zeros((1, 128), F32)] * (16 - members - 1)
        return total + jnp.concatenate(lines, 0)

    total = jnp.zeros((members * 16, 128), F32)
    if owners == group:
        total = gram(0, total)
    else:
        total = lax.fori_loop(0, owners // group, gram, total)
    sums = jnp.sum(total, axis=1, keepdims=True)
    spot = lax.broadcasted_iota(I32, (members, 16, 128), 1) == lax.broadcasted_iota(
        I32, (members, 16, 128), 2
    )
    near_ref[mem] = jnp.sum(jnp.where(spot, sums.reshape(members, 16, 1), 0.0), axis=1)

    def near_copy(d, slot):
        return mem_copy(d, near_ref.at[mem], near_ref.at[slot], near_send, near_recv)

    for d in range(1, mem_count):
        near_copy(d, mem).start()

    def wait_base(d, carry):
        base_copy(d, (plane + owners - d) % owners).wait()
        return carry

    lax.fori_loop(1, owners, wait_base, 0)
    position, _ = lines_of(message_ref[plane, 3 * each :], records)

    def spread(chunk, total):
        cells = base_got[pl.ds(chunk * group, group)].reshape(group * slots, 128)
        at = lax.broadcasted_iota(I32, (group * slots, records), 0) + chunk * (group * slots)
        hot = jnp.where(at.astype(F32) == position, 1.0, 0.0).astype(BF)
        return total + lax.dot_general(
            cells, hot, (((0,), (0,)), ((), ())), preferred_element_type=F32
        )

    def misfit():
        picked = jnp.zeros((128, records), F32)
        if owners == group:
            picked = spread(0, picked)
        else:
            picked = lax.fori_loop(0, owners // group, spread, picked)
        deeper = pltpu.roll(picked, 127, 0)
        level = lax.broadcasted_iota(I32, (128, 1), 0)
        deeper = jnp.where(level == levels - 1, picked, deeper)
        for fetch in fetches:
            fetch.wait()
        weight = w_ref[...]
        misfit_ref[...] = obs_ref[...] - (
            weight * picked[:levels] + (1.0 - weight) * deeper[:levels]
        )

    for d in range(1, mem_count):
        near_copy(d, mem).wait_send()
        near_copy(d, (mem + mem_count - d) % mem_count).wait_recv()
    tiles_ref[plane] = jnp.sum(near_ref[...], axis=0)

    def sum_copy(d, slot):
        return plane_copy(d, tiles_ref.at[plane], tiles_ref.at[slot], sum_send, sum_recv)

    def start_sum(d, carry):
        sum_copy(d, plane).start()
        return carry

    def wait_sum(d, carry):
        sum_copy(d, plane).wait_send()
        sum_copy(d, (plane + owners - d) % owners).wait_recv()
        return carry

    lax.fori_loop(1, owners, start_sum, 0)
    misfit()
    lax.fori_loop(1, owners, wait_sum, 0)
    sum_ref[...] = jnp.sum(tiles_ref[...], axis=0) * (1.0 / (records * owners * levels))


def last_kernel(
    sum_ref, misfit_ref, gram_at, projection_at, misfit_at, gram_ref, projection_ref, sem
):
    members = sum_ref.shape[0]
    total = sum_ref[...]
    across = lax.broadcasted_iota(I32, (members, 128), 1)
    down = lax.broadcasted_iota(I32, (members, 128), 0)
    gram_ref[...] = total[:, :members]
    row = jnp.sum(
        jnp.where(across == down, total[:, members : members + 1], 0.0), axis=0, keepdims=True
    )
    projection_ref[...] = row[:, :members]
    copies = [
        pltpu.make_async_copy(misfit_ref, misfit_at, sem.at[0]),
        pltpu.make_async_copy(gram_ref, gram_at, sem.at[1]),
        pltpu.make_async_copy(projection_ref, projection_at, sem.at[2]),
    ]
    for copy in copies:
        copy.start()
    for copy in copies:
        copy.wait()


def hbm(count):
    return [pl.BlockSpec(memory_space=pltpu.HBM)] * count


def vmem(count):
    return [pl.BlockSpec(memory_space=pltpu.VMEM)] * count


def on_device(
    mesh, initial_temp, land_mask, pert_table, pert_index, base_kh, member_mix, base_mix, owner,
    column, interp_w, obs_inv_var, observed,
):
    mem_count, lat_count, lon_count = (mesh.shape[a] for a in ("mem", "lat", "lon"))
    owners = lat_count * lon_count
    levels, width, length = initial_temp.shape
    local = member_mix.shape[0]
    runs, records = local + 1, owner.shape[0]
    rows = up(levels + 1, 16)
    capacity = max(2, 2 * records // owners)
    slots = up(capacity, 16 * mem_count)
    each = slots // mem_count
    offsets, ring = offsets_of(lon_count, width)
    columns = len(offsets) * width
    plans, blocks = lat_blocks(columns, ring, length)
    total = len(plans)
    own = width * length
    limit = pltpu.CompilerParams(vmem_limit_bytes=48 << 20)

    w, inv_var, measured = interp_w.T, obs_inv_var.T, observed.T
    dma = pltpu.SemaphoreType.DMA
    near_count = max(1, len(offsets) - 1)
    main, near, halo, messages = pl.pallas_call(
        functools.partial(exchange_kernel, (lat_count, lon_count, offsets, slots, each)),
        out_shape=(
            jax.ShapeDtypeStruct((rows, own), BF),
            jax.ShapeDtypeStruct((near_count, rows, own), BF),
            jax.ShapeDtypeStruct((len(offsets), 2, rows, 128), BF),
            jax.ShapeDtypeStruct((owners, 3 * each + 16, 128), BF),
        ),
        in_specs=hbm(7),
        out_specs=tuple(vmem(4)),
        scratch_shapes=[
            pltpu.VMEM((rows, own), F32),
            pltpu.VMEM((rows, 128), BF),
            pltpu.VMEM((owners, 3 * each + 16, 128), BF),
            pltpu.VMEM((levels, width, length), F32),
            pltpu.VMEM((width, length), I32),
            pltpu.VMEM((1, records), I32),
            pltpu.VMEM((1, records), I32),
            pltpu.VMEM((levels, records), F32),
            pltpu.VMEM((levels, records), F32),
            pltpu.VMEM((levels, records), F32),
            dma((7,)),
            dma((near_count,)), dma((near_count,)),
            dma((len(offsets), 2)), dma((len(offsets), 2)),
            dma((owners - 1,)), dma((owners - 1,)),
        ],
        compiler_params=pltpu.CompilerParams(
            collective_id=0, has_side_effects=True, vmem_limit_bytes=48 << 20
        ),
    )(
        initial_temp, land_mask, owner.reshape(1, records), column.reshape(1, records),
        w, inv_var, measured,
    )

    final, final_base, picks, base = pl.pallas_call(
        functools.partial(
            steps_kernel, (lat_count, lon_count, offsets, ring, slots, mem_count, records), plans
        ),
        out_shape=(
            jax.ShapeDtypeStruct((local, levels, width, length), BF),
            jax.ShapeDtypeStruct((levels, width, length), BF),
            jax.ShapeDtypeStruct((mem_count, owners, local, each, 128), BF),
            jax.ShapeDtypeStruct((owners, slots, 128), BF),
        ),
        in_specs=[pl.BlockSpec(memory_space=pltpu.SMEM)] + vmem(6) + hbm(3),
        out_specs=tuple(hbm(2) + vmem(2)),
        scratch_shapes=[
            pltpu.VMEM((runs * rows, total * 128), BF),
            pltpu.VMEM((runs * rows, total * 128), BF),
            pltpu.VMEM((runs * 128, own), BF),
            pltpu.VMEM(blocks.shape, BF),
            pltpu.VMEM(pert_table.shape, F32),
            pltpu.VMEM((1, levels), F32),
            pltpu.VMEM((runs, levels, width, length), F32),
            pltpu.VMEM((runs, levels, width, length), BF),
            dma((3,)),
            dma((runs,)),
        ],
        compiler_params=limit,
    )(
        pert_index, main, near, halo, messages, member_mix, base_mix,
        jnp.asarray(blocks, BF), pert_table, base_kh.reshape(1, levels),
    )

    sums, misfit = pl.pallas_call(
        functools.partial(gram_kernel, (mem_count, lat_count, lon_count, slots)),
        out_shape=(
            jax.ShapeDtypeStruct((local * mem_count, 128), F32),
            jax.ShapeDtypeStruct((levels, records), F32),
        ),
        in_specs=vmem(3) + hbm(2),
        out_specs=tuple(vmem(2)),
        scratch_shapes=[
            pltpu.VMEM((levels, records), F32),
            pltpu.VMEM((levels, records), F32),
            dma((2,)),
            pltpu.VMEM((mem_count, owners, local, each, 128), BF),
            pltpu.VMEM((owners, slots, 128), BF),
            pltpu.VMEM((mem_count, local * mem_count, 128), F32),
            pltpu.VMEM((owners, local * mem_count, 128), F32),
            dma((mem_count - 1,)), dma((mem_count - 1,)),
            dma((owners - 1,)), dma((owners - 1,)),
            dma((mem_count - 1,)), dma((mem_count - 1,)),
            dma((owners - 1,)), dma((owners - 1,)),
        ],
        compiler_params=pltpu.CompilerParams(
            collective_id=1, has_side_effects=True, vmem_limit_bytes=48 << 20
        ),
    )(picks, base, messages, w, measured)

    members = local * mem_count
    gram, projection, misfit = pl.pallas_call(
        last_kernel,
        out_shape=(
            jax.ShapeDtypeStruct((members, members), F32),
            jax.ShapeDtypeStruct((1, members), F32),
            jax.ShapeDtypeStruct((levels, records), F32),
        ),
        in_specs=vmem(2),
        out_specs=tuple(hbm(3)),
        scratch_shapes=[
            pltpu.VMEM((members, members), F32), pltpu.VMEM((1, members), F32), dma((3,)),
        ],
        compiler_params=limit,
    )(sums, misfit)
    return (final, final_base, gram, projection.reshape(members), misfit.T)


def solution(mesh):
    placed = (
        P(None, "lon", "lat"),
        P("lon", "lat"),
        P(),
        P("mem"),
        P(),
        P("mem", None, None),
        P(),
        P(("lat", "lon"), None),
        P(("lat", "lon")),
        P(("lat", "lon"), None),
        P(("lat", "lon"), None),
        P(("lat", "lon"), None),
    )
    return jax.shard_map(
        functools.partial(on_device, mesh),
        mesh=mesh,
        in_specs=placed,
        out_specs=(
            P("mem", None, "lon", "lat"),
            P(None, "lon", "lat"),
            P(),
            P(),
            P(("lat", "lon"), None),
        ),
        check_vma=False,
    )
```
